128 devices in a mesh: curve: 64 (over z, y, x), aux: 2 (over core).
Axes of the slice: x: 4, y: 4, z: 4, core: 2. Of those that a mesh axis runs over, the one named last changes fastest.
Arguments:
- coeffs: bfloat16 [128, 12800, 320], P('curve', 'aux'), may hold values from -6 to 6
- kernel: bfloat16 [512, 320, 320], P('curve'), may hold values from -0.3125 to 0.3125
- metric: float32 [128, 12800], P(None, 'aux'), may hold values from 0.5 to 2
- counts: int32 [128], replicated, may hold values from 6500 to 12800, as said below
- pairs: int32 [512, 2], P('curve'), may hold values from 0 to 127, as said below
Outputs:
- exchange: float32 [128, 320, 320], P('curve', 'aux')
The draws below stay inside these ranges and needn't reach their ends.
Inputs may be any that keep to these rules, and one draw needn't show every extreme that they name: counts are 100 times a block's atom count; some block has all 12800. `pairs`: rows 8 * d to 8 * d + 7 name as first block one of blocks 2 * d to 2 * d + 1 and as second block one of blocks 2 * d - 2 to 2 * d + 2 * 2 - 1; every existing block of that range is named by some row of these.
All inputs are finite; a program needn't handle non-finite values.
Results may differ from the reference program's by a relative error of at most 0.0025.
Values may be sent and summed in bfloat16 or wider, within the bound.
A program may use at most 128 MiB of HBM per device.

```python
import math
import jax
import jax.numpy as jnp
from jax import lax

ATOMS = 128
AUX_ATOM = 100
NG = 320
BPD = 2
AUXB = 12800
PPD = 8
NBLK = 128
NPAIR = 512
N_CURVE = 64


def draw_counts(key, part):
    key = jax.random.fold_in(key, 11)
    key_atoms, key_top = jax.random.split(key)
    atoms = jax.random.randint(key_atoms, (NBLK,), ATOMS // 2 + 1, ATOMS + 1)
    top = jax.random.randint(key_top, (), 0, NBLK)
    atoms = atoms.at[top].set(ATOMS)
    return (atoms * AUX_ATOM).astype(jnp.int32)


def draw_pairs(key, part):
    key = jax.random.fold_in(key, 23)
    key_local, key_order, key_first = jax.random.split(key, 3)
    span = 3 * BPD
    slots = jnp.arange(PPD, dtype=jnp.int32)[None, :]
    extra = jax.random.randint(key_local, (N_CURVE, PPD), 0, span)
    local = jnp.where(slots < span, slots, extra)
    scores = jax.random.randint(key_order, (N_CURVE, PPD), 0, 2 ** 20) * PPD + slots
    order = jnp.argsort(scores, axis=1, stable=True)
    local = jnp.take_along_axis(local, order, axis=1)
    device = jnp.arange(N_CURVE, dtype=jnp.int32)[:, None]
    second = device * BPD - BPD + local
    outside = (second < 0) | (second >= NBLK)
    second = jnp.where(outside, device * BPD + local % BPD, second)
    first = device * BPD + jax.random.randint(key_first, (N_CURVE, PPD), 0, BPD)
    return jnp.stack([first, second], axis=-1).reshape(NPAIR, 2).astype(jnp.int32)


def block_levels(rng, dims, pieces, low, largest):
    def one(position, blocks):
        draws = jax.random.uniform(jax.random.fold_in(jax.random.fold_in(rng, 6), position), (blocks,), jnp.float32, low / len(pieces), largest / len(pieces))
        return jnp.repeat(jnp.exp(draws), dims[position] // blocks).reshape((-1,) + (1,) * (len(dims) - position - 1))

    factor_of = one(*pieces[0])
    for cut in pieces[1:]:
        factor_of = factor_of * one(*cut)
    return factor_of


def gaussian(rng, dims, scale, most, cuts=(), held_as=jnp.bfloat16):
    values = jax.random.normal(rng, dims, jnp.float32) * scale
    if len(cuts) > 0:
        values = block_levels(rng, dims, cuts, -0.22, 0.18) * values
    return jnp.clip(values, min=-most, max=most).astype(held_as)


def setup_inputs(seed: int = 0) -> dict:
    arg_keys = jax.random.split(jax.random.key(seed), 6)
    coeffs = gaussian(arg_keys[0], (NBLK, AUXB, NG), 1.0, 6.0, ((0, 64), (1, 2)))
    kernel = gaussian(arg_keys[1], (NPAIR, NG, NG), NG ** -0.5, 0.3125, ((0, 64),))
    metric = jnp.clip(jnp.exp(math.log(2.0) - 1.3862944 * jax.random.uniform(arg_keys[2], (NBLK, AUXB), jnp.float32) ** block_levels(arg_keys[2], (NBLK, AUXB), ((1, 2),), -0.2, 0.2)), 0.5, 2.0)
    counts = draw_counts(jax.random.fold_in(arg_keys[5], 71), 0)
    pairs = draw_pairs(jax.random.fold_in(arg_keys[5], 71), 0)
    return dict(coeffs=coeffs, kernel=kernel, metric=metric, counts=counts, pairs=pairs)


def reference(coeffs, kernel, metric, counts, pairs):
    rows = jnp.arange(AUXB, dtype=jnp.int32)

    def step(acc, item):
        kblock, pair = item
        first = pair[0]
        second = pair[1]
        ca = coeffs[first]
        cb = coeffs[second]
        left = jnp.dot(ca, kblock, preferred_element_type=jnp.float32)
        density = jnp.sum(left * cb.astype(jnp.float32), axis=1)
        live = rows < jnp.minimum(counts[first], counts[second])
        weight = jnp.where(live, metric[first] * metric[second] * density * (NG ** -0.5), jnp.float32(0.0))
        scaled = (weight[:, None] * cb.astype(jnp.float32)).astype(jnp.bfloat16)
        block = jnp.dot(ca.T, scaled, preferred_element_type=jnp.float32) * (AUXB ** -0.5)
        acc = acc.at[first].add(block)
        acc = acc.at[second].add(block.T)
        return acc, None

    start = jnp.zeros((coeffs.shape[0], NG, NG), jnp.float32)
    result, _ = lax.scan(step, start, (kernel, pairs))
    return result
```

```python
import functools

import jax
import jax.numpy as jnp
from jax import lax
from jax.experimental import pallas as pl
from jax.experimental.pallas import tpu as pltpu
from jax.sharding import PartitionSpec as P

MESH = pl.DeviceIdType.MESH
NG = 320
AUXB = 12800
ROWS = 6400
HALF = 3200
PART = 640
PARTS = HALF // PART
PAIRS = 8
RING = 64
NBLK = 128
OUT = NG // 2
F32 = jnp.float32
BF16 = jnp.bfloat16


def across(a, b):
    return lax.dot_general(a, b, (((1,), (1,)), ((), ())), preferred_element_type=F32)


def body(
    coeffs, kernel, metric, counts, pairs, out,
    own, got, blocks, met, sums, sent_k, got_k, mix, mix_own, weight_own, zs, acc,
    got_pair, send_res, got_res,
    load_sem, row_send, row_recv, k_send, k_recv, kf_send, kf_recv,
    pair_send, pair_recv, res_send, res_recv,
):
    here = lax.axis_index("curve")
    core = lax.axis_index("aux")
    after = lax.rem(here + 1, RING)
    before = lax.rem(here + RING - 1, RING)
    sides = ((before, core), (after, core))
    twin = (here, 1 - core)

    barrier = pltpu.get_barrier_semaphore()
    for target in (*sides, twin):
        pl.semaphore_signal(barrier, inc=1, device_id=target, device_id_type=MESH)

    loads = [
        pltpu.make_async_copy(kernel, blocks, load_sem.at[0]),
        pltpu.make_async_copy(metric, met, load_sem.at[1]),
        pltpu.make_async_copy(coeffs, own, load_sem.at[2]),
    ]
    for load in loads:
        load.start()
    loads[0].wait()

    first = [pairs[p, 0] - 2 * here for p in range(PAIRS)]
    second = [pairs[p, 1] - 2 * here + 2 for p in range(PAIRS)]

    def add_kernels(index, _):
        i = index // 6
        s = index % 6
        named = [(first[p] == i) & (second[p] == s) for p in range(PAIRS)]

        def rows(r, _):
            at = pl.ds(pl.multiple_of(r * 64, 64), 64)
            total = jnp.zeros((64, NG), F32)
            for p in range(PAIRS):
                total = total + jnp.where(named[p], blocks[p, at, :].astype(F32), 0.0)
            sums[index, at, :] = total
            return 0

        return lax.fori_loop(0, NG // 64, rows, 0)

    lax.fori_loop(0, 12, add_kernels, 0)

    for e in range(2):
        for j in range(2):
            sent_k[e, j] = sums[6 * core + 4 * e + j].astype(BF16)

    pl.semaphore_wait(barrier, 3)

    def k_copy(e):
        return pltpu.make_async_remote_copy(
            src_ref=sent_k.at[e],
            dst_ref=got_k.at[1 - e, core],
            send_sem=k_send.at[e],
            recv_sem=k_recv.at[1 - e],
            device_id=sides[e],
            device_id_type=MESH,
        )

    def k_forward(e):
        return pltpu.make_async_remote_copy(
            src_ref=got_k.at[e, core],
            dst_ref=got_k.at[e, core],
            send_sem=kf_send.at[e],
            recv_sem=kf_recv.at[e],
            device_id=twin,
            device_id_type=MESH,
        )

    def row_copy(e, k):
        start = (1 - e) * HALF if e == 0 else 0
        start = start + k * PART
        at = pl.ds(pl.multiple_of(start, 128), PART)
        to = pl.ds(pl.multiple_of(k * PART, 128), PART)
        return pltpu.make_async_remote_copy(
            src_ref=coeffs.at[:, :, at],
            dst_ref=got.at[1 - e, :, :, to],
            send_sem=row_send.at[e, k],
            recv_sem=row_recv.at[1 - e, k],
            device_id=sides[e],
            device_id_type=MESH,
        )

    def row_wait(e, k):
        row_copy(1 - e, k).wait_recv()

    for e in range(2):
        k_copy(e).start()
    for k in range(2):
        for e in range(2):
            row_copy(e, k).start()

    eye = (
        lax.broadcasted_iota(jnp.int32, (NG, NG), 0)
        == lax.broadcasted_iota(jnp.int32, (NG, NG), 1)
    ).astype(BF16)
    loads[1].wait()
    loads[2].wait()
    mix_own[0] = sums[2].astype(BF16)
    mix_own[2] = sums[9].astype(BF16)
    mix_own[1] = (sums[3] + across(eye, sums[8].astype(BF16))).astype(BF16)

    block_of = [lax.rem(2 * here + NBLK - 2 + s, NBLK) for s in range(6)]
    count_of = [counts[block_of[s]] for s in range(6)]

    def factor(s, t, start, size):
        at = pl.ds(pl.multiple_of(start, 128), size)
        a = met[pl.ds(block_of[s], 1), at]
        b = met[pl.ds(block_of[t], 1), at]
        row = core * ROWS + start + lax.broadcasted_iota(jnp.int32, (1, size), 1)
        live = row < jnp.minimum(count_of[s], count_of[t])
        return live, a * b * NG ** (-0.5)

    def own_part(k, _):
        start = pl.multiple_of(k * PART, 128)
        at = pl.ds(start, PART)
        for index, (i, j) in enumerate(((0, 0), (0, 1), (1, 1))):
            left = jnp.dot(mix_own[index], own[j, :, at], preferred_element_type=F32)
            density = jnp.sum(left * own[i, :, at].astype(F32), axis=0, keepdims=True)
            live, scale = factor(2 + i, 2 + j, start, PART)
            weight_own[pl.ds(index, 1), at] = jnp.where(live, scale * density, 0.0)
        return 0

    lax.fori_loop(0, ROWS // PART, own_part, 0)

    for e in range(2):
        k_copy(1 - e).wait_recv()
        k_forward(e).start()
    for e in range(2):
        pltpu.make_async_remote_copy(
            src_ref=got_k.at[e, core],
            dst_ref=got_k.at[e, 1 - core],
            send_sem=kf_send.at[e],
            recv_sem=kf_recv.at[e],
            device_id=twin,
            device_id_type=MESH,
        ).wait_recv()
        for j in range(2):
            for i in range(2):
                turned = across(eye, got_k[e, j, i])
                mix[e, j, i * NG:(i + 1) * NG, :] = (sums[6 * i + 4 * e + j] + turned).astype(BF16)

    acc[...] = jnp.zeros_like(acc)

    def put(slot, value):
        high = value.astype(BF16)
        zs[slot, 0] = high
        zs[slot, 1] = (value - high.astype(F32)).astype(BF16)

    def edge(e, k):
        start = e * HALF + k * PART
        at = pl.ds(pl.multiple_of(start, 128), PART)
        to = pl.ds(pl.multiple_of(k * PART, 128), PART)
        y = [own[i, :, at].astype(F32) for i in range(2)]
        weights = []
        for j in range(2):
            left = jnp.dot(mix[e, j], got[e, j, :, to], preferred_element_type=F32)
            each = []
            for i in range(2):
                density = jnp.sum(left[i * NG:(i + 1) * NG] * y[i], axis=0, keepdims=True)
                live, scale = factor(2 + i, 4 * e + j, start, PART)
                each.append(jnp.where(live, scale * density, 0.0))
            weights.append(each)
        mine = [weight_own[pl.ds(index, 1), at] for index in range(3)]
        x = [got[e, j, :, to].astype(F32) for j in range(2)]
        put(0, weights[0][0] * x[0] + weights[1][0] * x[1] + 2.0 * mine[0] * y[0] + mine[1] * y[1])
        put(1, weights[0][1] * x[0] + weights[1][1] * x[1] + mine[1] * y[0] + 2.0 * mine[2] * y[1])
        for j in range(2):
            put(2 + j, weights[j][0] * y[0] + weights[j][1] * y[1])
        for i in range(2):
            rows = own[i, :, at]
            acc[i] += across(rows, zs[i, 0]) + across(rows, zs[i, 1])
        for j in range(2):
            rows = got[e, j, :, to]
            acc[2 + 2 * e + j] += across(rows, zs[2 + j, 0]) + across(rows, zs[2 + j, 1])

    def step(k, _):
        for e in range(2):
            row_copy(e, k).wait_send()

            @pl.when(k + 2 < PARTS)
            def _():
                row_copy(e, k + 2).start()

        for e in range(2):
            row_wait(e, k)
            edge(e, k)
        return 0

    lax.fori_loop(0, PARTS, step, 0)

    keep = pl.ds(pl.multiple_of(core * OUT, 32), OUT)
    give = pl.ds(pl.multiple_of((1 - core) * OUT, 32), OUT)
    order = ((2, 2), (4, 2), (0, 2))
    swaps = [
        pltpu.make_async_remote_copy(
            src_ref=acc.at[pl.ds(start, size), give],
            dst_ref=got_pair.at[pl.ds(start, size)],
            send_sem=pair_send.at[n],
            recv_sem=pair_recv.at[n],
            device_id=twin,
            device_id_type=MESH,
        )
        for n, (start, size) in enumerate(order)
    ]
    for swap in swaps:
        swap.start()
    results = [
        pltpu.make_async_remote_copy(
            src_ref=send_res.at[e],
            dst_ref=got_res.at[1 - e],
            send_sem=res_send.at[e],
            recv_sem=res_recv.at[1 - e],
            device_id=sides[e],
            device_id_type=MESH,
        )
        for e in range(2)
    ]
    norm = AUXB ** (-0.5)
    for e in range(2):
        swaps[e].wait_recv()
        for j in range(2):
            total = acc[2 + 2 * e + j, keep, :] + got_pair[2 + 2 * e + j]
            send_res[e, j] = (total * norm).astype(BF16)
        results[e].start()
    swaps[2].wait_recv()
    for i in range(2):
        out[i] = (acc[i, keep, :] + got_pair[i]) * norm
    for e in range(2):
        results[1 - e].wait_recv()
        for i in range(2):
            out[i] += got_res[e, i].astype(F32)
    for e in range(2):
        k_copy(e).wait_send()
        k_forward(e).wait_send()
        results[e].wait_send()
    for swap in swaps:
        swap.wait_send()


def shards(coeffs, kernel, metric, counts, pairs):
    anywhere = pl.BlockSpec(memory_space=pl.ANY)
    scalars = pl.BlockSpec(memory_space=pltpu.SMEM)
    dma = pltpu.SemaphoreType.DMA
    return pl.pallas_call(
        body,
        out_shape=jax.ShapeDtypeStruct((2, OUT, NG), F32),
        in_specs=[anywhere, anywhere, anywhere, scalars, scalars],
        out_specs=pl.BlockSpec(memory_space=pltpu.VMEM),
        scratch_shapes=[
            pltpu.VMEM((2, NG, ROWS), BF16),
            pltpu.VMEM((2, 2, NG, HALF), BF16),
            pltpu.VMEM((PAIRS, NG, NG), BF16),
            pltpu.VMEM((NBLK, ROWS), F32),
            pltpu.VMEM((12, NG, NG), F32),
            pltpu.VMEM((2, 2, NG, NG), BF16),
            pltpu.VMEM((2, 2, 2, NG, NG), BF16),
            pltpu.VMEM((2, 2, 2 * NG, NG), BF16),
            pltpu.VMEM((3, NG, NG), BF16),
            pltpu.VMEM((8, ROWS), F32),
            pltpu.VMEM((4, 2, NG, PART), BF16),
            pltpu.VMEM((6, NG, NG), F32),
            pltpu.VMEM((6, OUT, NG), F32),
            pltpu.VMEM((2, 2, OUT, NG), BF16),
            pltpu.VMEM((2, 2, OUT, NG), BF16),
            dma((3,)),
            dma((2, PARTS)),
            dma((2, PARTS)),
            dma((2,)),
            dma((2,)),
            dma((2,)),
            dma((2,)),
            dma((3,)),
            dma((3,)),
            dma((2,)),
            dma((2,)),
        ],
        compiler_params=pltpu.CompilerParams(
            collective_id=0, has_side_effects=True, vmem_limit_bytes=58 * 2 ** 20
        ),
        cost_estimate=pl.CostEstimate(
            flops=30 * 10 ** 9, bytes_accessed=14 * 10 ** 6, transcendentals=0
        ),
    )(jnp.transpose(coeffs, (0, 2, 1)), kernel, metric, counts, pairs)


def solution(mesh):
    in_specs = (
        P("curve", "aux", None),
        P("curve", None, None),
        P(None, "aux"),
        P(),
        P("curve", None),
    )
    out_specs = P("curve", "aux", None)
    return jax.shard_map(shards, mesh=mesh, in_specs=in_specs, out_specs=out_specs, check_vma=False)
```

```python
import functools

import jax
import jax.numpy as jnp
from jax import lax
from jax.experimental import pallas as pl
from jax.experimental.pallas import tpu as pltpu
from jax.sharding import PartitionSpec as P

MESH = pl.DeviceIdType.MESH
NG = 320
AUXB = 12800
ROWS = 6400
BOTH = 256
ONE = (ROWS - BOTH) // 2
PART = 512
PARTS = 5
OWN_PART = 640
LAST = (384, 128)
SIZES = (PART,) * PARTS + LAST + (BOTH,)
STARTS = tuple(sum(SIZES[:k]) for k in range(len(SIZES)))
COPIES = len(SIZES)
PAIRS = 8
RING = 64
NBLK = 128
OUT = NG // 2
F32 = jnp.float32
BF16 = jnp.bfloat16


def across(a, b):
    return lax.dot_general(a, b, (((1,), (1,)), ((), ())), preferred_element_type=F32)


def body(
    coeffs, kernel, metric, counts, pairs, out,
    own, got, blocks, met, near, sums, sent_k, got_k, mix, mix_own, weight_own, zs, acc,
    got_pair, send_res, got_res,
    load_sem, row_send, row_recv, k_send, k_recv, kf_send, kf_recv,
    pair_send, pair_recv, res_send, res_recv,
):
    here = lax.axis_index("curve")
    core = lax.axis_index("aux")
    after = lax.rem(here + 1, RING)
    before = lax.rem(here + RING - 1, RING)
    sides = ((before, core), (after, core))
    twin = (here, 1 - core)

    barrier = pltpu.get_barrier_semaphore()
    for target in (*sides, twin):
        pl.semaphore_signal(barrier, inc=1, device_id=target, device_id_type=MESH)

    loads = [
        pltpu.make_async_copy(kernel, blocks, load_sem.at[0]),
        pltpu.make_async_copy(metric, met, load_sem.at[1]),
        pltpu.make_async_copy(coeffs, own, load_sem.at[2]),
    ]
    for load in loads:
        load.start()
    pl.semaphore_wait(barrier, 3)

    def k_copy(e):
        return pltpu.make_async_remote_copy(
            src_ref=sent_k.at[e],
            dst_ref=got_k.at[1 - e, core],
            send_sem=k_send.at[e],
            recv_sem=k_recv.at[1 - e],
            device_id=sides[e],
            device_id_type=MESH,
        )

    def k_forward(e):
        return pltpu.make_async_remote_copy(
            src_ref=got_k.at[e, core],
            dst_ref=got_k.at[e, core],
            send_sem=kf_send.at[e],
            recv_sem=kf_recv.at[e],
            device_id=twin,
            device_id_type=MESH,
        )

    def there(e, start):
        if isinstance(start, int):
            return start + (ONE + BOTH) * (e == 1 and start < ONE)
        return pl.multiple_of(start + (ONE + BOTH) * e, 128)

    def row_copy(e, k):
        if isinstance(k, int):
            start, size = STARTS[k], SIZES[k]
        else:
            start, size = pl.multiple_of(k * PART, 128), PART
        return pltpu.make_async_remote_copy(
            src_ref=coeffs.at[:, :, pl.ds(there(1 - e, start), size)],
            dst_ref=got.at[1 - e, :, :, pl.ds(start, size)],
            send_sem=row_send.at[e, k],
            recv_sem=row_recv.at[1 - e, k],
            device_id=sides[e],
            device_id_type=MESH,
        )

    for e in range(2):
        row_copy(e, 0).start()
    loads[0].wait()

    first = [pairs[0, p] - 2 * here for p in range(PAIRS)]
    second = [pairs[1, p] - 2 * here + 2 for p in range(PAIRS)]

    def add_kernels(index, _):
        i = index // 6
        s = index % 6
        named = [(first[p] == i) & (second[p] == s) for p in range(PAIRS)]

        def rows(r, _):
            at = pl.ds(pl.multiple_of(r * 64, 64), 64)
            total = jnp.zeros((64, NG), F32)
            for p in range(PAIRS):
                total = total + jnp.where(named[p], blocks[p, at, :].astype(F32), 0.0)
            sums[index, at, :] = total
            return 0

        return lax.fori_loop(0, NG // 64, rows, 0)

    lax.fori_loop(0, 12, add_kernels, 0)


    for e in range(2):
        both = [sums[6 * core + 4 * e + j].astype(BF16) for j in range(2)]
        sent_k[e] = jnp.concatenate(both, axis=1)
        k_copy(e).start()
    for e in range(2):
        row_copy(e, 1).start()

    wide_eye = (
        lax.broadcasted_iota(jnp.int32, (2 * NG, 2 * NG), 0)
        == lax.broadcasted_iota(jnp.int32, (2 * NG, 2 * NG), 1)
    ).astype(BF16)
    eye = wide_eye[:NG, :NG]
    loads[1].wait()
    loads[2].wait()
    mix_own[0] = sums[2].astype(BF16)
    mix_own[2] = sums[9].astype(BF16)
    mix_own[1] = (sums[3] + across(eye, sums[8].astype(BF16))).astype(BF16)

    block_of = [lax.rem(2 * here + NBLK - 2 + s, NBLK) for s in range(6)]
    count_of = [counts[block_of[s]] for s in range(6)]
    for s in range(6):
        near[s:s + 1, :] = met[pl.ds(block_of[s], 1), :]

    def factor(s, t, start, size):
        at = pl.ds(pl.multiple_of(start, 128), size)
        a = near[s:s + 1, at]
        b = near[t:t + 1, at]
        row = core * ROWS + start + lax.broadcasted_iota(jnp.int32, (1, size), 1)
        live = row < jnp.minimum(count_of[s], count_of[t])
        return live, a * b * NG ** (-0.5)

    def own_part(k, _):
        start = pl.multiple_of(k * OWN_PART, 128)
        at = pl.ds(start, OWN_PART)
        for index, (i, j) in enumerate(((0, 0), (0, 1), (1, 1))):
            left = jnp.dot(mix_own[index], own[j, :, at], preferred_element_type=F32)
            density = jnp.sum(left * own[i, :, at].astype(F32), axis=0, keepdims=True)
            live, scale = factor(2 + i, 2 + j, start, OWN_PART)
            weight_own[pl.ds(index, 1), at] = jnp.where(live, scale * density, 0.0)
        return 0

    lax.fori_loop(0, ROWS // OWN_PART, own_part, 0)

    for e in range(2):
        k_copy(1 - e).wait_recv()
        k_forward(e).start()
    for e in range(2):
        pltpu.make_async_remote_copy(
            src_ref=got_k.at[e, core],
            dst_ref=got_k.at[e, 1 - core],
            send_sem=kf_send.at[e],
            recv_sem=kf_recv.at[e],
            device_id=twin,
            device_id_type=MESH,
        ).wait_recv()
        for j in range(2):
            turned = across(wide_eye, got_k[e, j])
            for i in range(2):
                at = pl.ds(i * NG, NG)
                mix[e, j, at, :] = (sums[6 * i + 4 * e + j] + turned[i * NG:(i + 1) * NG]).astype(BF16)

    acc[...] = jnp.zeros_like(acc)

    def put(e, slot, size, value):
        high = value.astype(BF16)
        zs[e, slot, 0, :, 0:size] = high
        zs[e, slot, 1, :, 0:size] = (value - high.astype(F32)).astype(BF16)

    def gram(e, slot, size, rows):
        return across(rows, zs[e, slot, 0, :, 0:size]) + across(rows, zs[e, slot, 1, :, 0:size])

    def weigh(e, start, size):
        mine_at = pl.ds(there(e, start), size)
        at = pl.ds(start, size)
        y = [own[i, :, mine_at].astype(F32) for i in range(2)]
        weights = []
        for j in range(2):
            left = jnp.dot(mix[e, j], got[e, j, :, at], preferred_element_type=F32)
            each = []
            for i in range(2):
                density = jnp.sum(left[i * NG:(i + 1) * NG] * y[i], axis=0, keepdims=True)
                live, scale = factor(2 + i, 4 * e + j, there(e, start), size)
                each.append(jnp.where(live, scale * density, 0.0))
            weights.append(each)
        return weights

    def from_own(start, size):
        at = pl.ds(start, size)
        y = [own[i, :, at].astype(F32) for i in range(2)]
        mine = [weight_own[pl.ds(index, 1), at] for index in range(3)]
        return (2.0 * mine[0] * y[0] + mine[1] * y[1], mine[1] * y[0] + 2.0 * mine[2] * y[1])

    def from_got(e, start, size, weights):
        x = [got[e, j, :, pl.ds(start, size)].astype(F32) for j in range(2)]
        return tuple(weights[0][i] * x[0] + weights[1][i] * x[1] for i in range(2))

    def one_way(e, start, size):
        weights = weigh(e, start, size)
        y = [own[i, :, pl.ds(there(e, start), size)].astype(F32) for i in range(2)]
        for j in range(2):
            put(e, 2 + j, size, weights[j][0] * y[0] + weights[j][1] * y[1])
        a = from_got(e, start, size, weights)
        b = from_own(there(e, start), size)
        for i in range(2):
            put(e, i, size, a[i] + b[i])

    def both_ways(start, size):
        a = from_got(0, start, size, weigh(0, start, size))
        b = from_got(1, start, size, weigh(1, start, size))
        c = from_own(start, size)
        for i in range(2):
            put(0, i, size, a[i] + b[i] + c[i])

    def add_theirs(e, start, size):
        for j in range(2):
            acc[2 + 2 * e + j] += gram(e, 2 + j, size, got[e, j, :, pl.ds(start, size)])

    def add_mine(e, start, size):
        for i in range(2):
            acc[i] += gram(e, i, size, own[i, :, pl.ds(there(e, start), size)])

    keep = pl.ds(pl.multiple_of(core * OUT, 32), OUT)
    give = pl.ds(pl.multiple_of((1 - core) * OUT, 32), OUT)
    swaps = [
        pltpu.make_async_remote_copy(
            src_ref=acc.at[pl.ds(start, 2), give],
            dst_ref=got_pair.at[pl.ds(start, 2)],
            send_sem=pair_send.at[n],
            recv_sem=pair_recv.at[n],
            device_id=twin,
            device_id_type=MESH,
        )
        for n, start in enumerate((2, 4, 0))
    ]

    def step(k, _):
        for e in range(2):
            row_copy(e, k).wait_send()

            @pl.when(k + 2 < PARTS)
            def _():
                row_copy(e, k + 2).start()

            for later in (PARTS, PARTS + 1):
                @pl.when(k + 2 == later)
                def _():
                    row_copy(e, later).start()

        for e in range(2):
            row_copy(1 - e, k).wait_recv()
            start = pl.multiple_of(k * PART, 128)
            one_way(e, start, PART)
            add_theirs(e, start, PART)
            add_mine(e, start, PART)
        return 0

    lax.fori_loop(0, PARTS, step, 0)

    for k in range(PARTS, COPIES - 1):
        for e in range(2):
            row_copy(e, k).wait_send()
            if k + 2 < COPIES:
                row_copy(e, k + 2).start()
        for e in range(2):
            row_copy(1 - e, k).wait_recv()
            one_way(e, STARTS[k], SIZES[k])
            add_theirs(e, STARTS[k], SIZES[k])
            if k == COPIES - 2:
                swaps[e].start()
            else:
                add_mine(e, STARTS[k], SIZES[k])
    for e in range(2):
        add_mine(e, STARTS[-2], SIZES[-2])

    results = [
        pltpu.make_async_remote_copy(
            src_ref=send_res.at[e],
            dst_ref=got_res.at[1 - e],
            send_sem=res_send.at[e],
            recv_sem=res_recv.at[1 - e],
            device_id=sides[e],
            device_id_type=MESH,
        )
        for e in range(2)
    ]
    norm = AUXB ** (-0.5)
    for e in range(2):
        swaps[e].wait_recv()
        both = [acc[2 + 2 * e + j, keep, :] + got_pair[2 + 2 * e + j] for j in range(2)]
        send_res[e] = jnp.concatenate([(total * norm).astype(BF16) for total in both], axis=1)
        results[e].start()
    for e in range(2):
        row_copy(e, COPIES - 1).wait_send()
        row_copy(1 - e, COPIES - 1).wait_recv()
    both_ways(STARTS[-1], BOTH)
    add_mine(0, STARTS[-1], BOTH)
    swaps[2].start()
    swaps[2].wait_recv()
    for i in range(2):
        out[i] = (acc[i, keep, :] + got_pair[i]) * norm
    for e in range(2):
        results[1 - e].wait_recv()
        for i in range(2):
            out[i] += got_res[e, :, i * NG:(i + 1) * NG].astype(F32)
    for e in range(2):
        k_copy(e).wait_send()
        k_forward(e).wait_send()
        results[e].wait_send()
    for swap in swaps:
        swap.wait_send()


def shards(coeffs, kernel, metric, counts, pairs):
    anywhere = pl.BlockSpec(memory_space=pl.ANY)
    scalars = pl.BlockSpec(memory_space=pltpu.SMEM)
    dma = pltpu.SemaphoreType.DMA
    return pl.pallas_call(
        body,
        out_shape=jax.ShapeDtypeStruct((2, OUT, NG), F32),
        in_specs=[anywhere, anywhere, anywhere, scalars, scalars],
        out_specs=pl.BlockSpec(memory_space=pltpu.VMEM),
        scratch_shapes=[
            pltpu.VMEM((2, NG, ROWS), BF16),
            pltpu.VMEM((2, 2, NG, ONE + BOTH), BF16),
            pltpu.VMEM((PAIRS, NG, NG), BF16),
            pltpu.VMEM((NBLK, ROWS), F32),
            pltpu.VMEM((8, ROWS), F32),
            pltpu.VMEM((12, NG, NG), F32),
            pltpu.VMEM((2, NG, 2 * NG), BF16),
            pltpu.VMEM((2, 2, NG, 2 * NG), BF16),
            pltpu.VMEM((2, 2, 2 * NG, NG), BF16),
            pltpu.VMEM((3, NG, NG), BF16),
            pltpu.VMEM((8, ROWS), F32),
            pltpu.VMEM((2, 4, 2, NG, PART), BF16),
            pltpu.VMEM((6, NG, NG), F32),
            pltpu.VMEM((6, OUT, NG), F32),
            pltpu.VMEM((2, OUT, 2 * NG), BF16),
            pltpu.VMEM((2, OUT, 2 * NG), BF16),
            dma((3,)),
            dma((2, COPIES)),
            dma((2, COPIES)),
            dma((2,)),
            dma((2,)),
            dma((2,)),
            dma((2,)),
            dma((3,)),
            dma((3,)),
            dma((2,)),
            dma((2,)),
        ],
        compiler_params=pltpu.CompilerParams(
            collective_id=0, has_side_effects=True, vmem_limit_bytes=58 * 2 ** 20
        ),
        cost_estimate=pl.CostEstimate(
            flops=30 * 10 ** 9, bytes_accessed=14 * 10 ** 6, transcendentals=0
        ),
    )(jnp.transpose(coeffs, (0, 2, 1)), kernel, metric, counts, jnp.transpose(pairs))


def solution(mesh):
    in_specs = (
        P("curve", "aux", None),
        P("curve", None, None),
        P(None, "aux"),
        P(),
        P("curve", None),
    )
    out_specs = P("curve", "aux", None)
    return jax.shard_map(shards, mesh=mesh, in_specs=in_specs, out_specs=out_specs, check_vma=False)
```

```python
import functools

import jax
import jax.numpy as jnp
from jax import lax
from jax.experimental import pallas as pl
from jax.experimental.pallas import tpu as pltpu
from jax.sharding import PartitionSpec as P

MESH = pl.DeviceIdType.MESH
NG = 320
AUXB = 12800
ROWS = 6400
BOTH = 256
ONE = (ROWS - BOTH) // 2
PART = 512
PARTS = 5
OWN_PART = 640
LAST = (384, 128)
SIZES = (PART,) * PARTS + LAST + (BOTH,)
STARTS = tuple(sum(SIZES[:k]) for k in range(len(SIZES)))
COPIES = len(SIZES)
PAIRS = 8
RING = 64
NBLK = 128
OUT = NG // 2
F32 = jnp.float32
BF16 = jnp.bfloat16


def across(a, b):
    return lax.dot_general(a, b, (((1,), (1,)), ((), ())), preferred_element_type=F32)


def body(
    coeffs, kernel, metric, counts, pairs, out,
    own, got, blocks, met, near, sums, sent_k, got_k, mix, mix_own, weight_own, zs, acc,
    got_pair, send_res, got_res,
    load_sem, row_send, row_recv, k_send, k_recv, kf_send, kf_recv,
    pair_send, pair_recv, res_send, res_recv,
):
    here = lax.axis_index("curve")
    core = lax.axis_index("aux")
    after = lax.rem(here + 1, RING)
    before = lax.rem(here + RING - 1, RING)
    sides = ((before, core), (after, core))
    twin = (here, 1 - core)
    there_is = (here > 0, here < RING - 1)

    def for_side(e):
        return pl.when(there_is[e])


    barrier = pltpu.get_barrier_semaphore()
    pl.semaphore_signal(barrier, inc=1, device_id=twin, device_id_type=MESH)
    for e in range(2):
        @for_side(e)
        def _():
            pl.semaphore_signal(barrier, inc=1, device_id=sides[e], device_id_type=MESH)

    loads = [
        pltpu.make_async_copy(kernel, blocks, load_sem.at[0]),
        pltpu.make_async_copy(metric, met, load_sem.at[1]),
        pltpu.make_async_copy(coeffs, own, load_sem.at[2]),
    ]
    for load in loads:
        load.start()

    for e in range(2):
        @pl.when(jnp.logical_not(there_is[e]))
        def _():
            got[e] = jnp.zeros_like(got[e])
            got_k[e] = jnp.zeros_like(got_k[e])
            got_res[e] = jnp.zeros_like(got_res[e])

    pl.semaphore_wait(barrier, 1 + there_is[0].astype(jnp.int32) + there_is[1].astype(jnp.int32))

    def k_copy(e):
        return pltpu.make_async_remote_copy(
            src_ref=sent_k.at[e],
            dst_ref=got_k.at[1 - e, core],
            send_sem=k_send.at[e],
            recv_sem=k_recv.at[1 - e],
            device_id=sides[e],
            device_id_type=MESH,
        )

    def k_forward(e):
        return pltpu.make_async_remote_copy(
            src_ref=got_k.at[e, core],
            dst_ref=got_k.at[e, core],
            send_sem=kf_send.at[e],
            recv_sem=kf_recv.at[e],
            device_id=twin,
            device_id_type=MESH,
        )

    def there(e, start):
        if isinstance(start, int):
            return start + (ONE + BOTH) * (e == 1 and start < ONE)
        return pl.multiple_of(start + (ONE + BOTH) * e, 128)

    def row_copy(e, k):
        if isinstance(k, int):
            start, size = STARTS[k], SIZES[k]
        else:
            start, size = pl.multiple_of(k * PART, 128), PART
        return pltpu.make_async_remote_copy(
            src_ref=coeffs.at[:, :, pl.ds(there(1 - e, start), size)],
            dst_ref=got.at[1 - e, :, :, pl.ds(start, size)],
            send_sem=row_send.at[e, k],
            recv_sem=row_recv.at[1 - e, k],
            device_id=sides[e],
            device_id_type=MESH,
        )

    def send_rows(e, k):
        @for_side(e)
        def _():
            row_copy(e, k).start()

    def rows_sent(e, k):
        @for_side(e)
        def _():
            row_copy(e, k).wait_send()

    def rows_here(e, k):
        @for_side(e)
        def _():
            row_copy(1 - e, k).wait_recv()

    for e in range(2):
        send_rows(e, 0)
    loads[0].wait()

    first = [pairs[0, p] - 2 * here for p in range(PAIRS)]
    second = [pairs[1, p] - 2 * here + 2 for p in range(PAIRS)]

    def add_kernels(index, _):
        i = index // 6
        s = index % 6
        named = [(first[p] == i) & (second[p] == s) for p in range(PAIRS)]

        def rows(r, _):
            at = pl.ds(pl.multiple_of(r * 64, 64), 64)
            total = jnp.zeros((64, NG), F32)
            for p in range(PAIRS):
                total = total + jnp.where(named[p], blocks[p, at, :].astype(F32), 0.0)
            sums[index, at, :] = total
            return 0

        return lax.fori_loop(0, NG // 64, rows, 0)

    lax.fori_loop(0, 12, add_kernels, 0)


    for e in range(2):
        both = [sums[6 * core + 4 * e + j].astype(BF16) for j in range(2)]
        sent_k[e] = jnp.concatenate(both, axis=1)

        @for_side(e)
        def _():
            k_copy(e).start()

    for e in range(2):
        send_rows(e, 1)

    wide_eye = (
        lax.broadcasted_iota(jnp.int32, (2 * NG, 2 * NG), 0)
        == lax.broadcasted_iota(jnp.int32, (2 * NG, 2 * NG), 1)
    ).astype(BF16)
    eye = wide_eye[:NG, :NG]
    loads[1].wait()
    loads[2].wait()
    mix_own[0] = sums[2].astype(BF16)
    mix_own[2] = sums[9].astype(BF16)
    mix_own[1] = (sums[3] + across(eye, sums[8].astype(BF16))).astype(BF16)

    block_of = [lax.rem(2 * here + NBLK - 2 + s, NBLK) for s in range(6)]
    count_of = [counts[block_of[s]] for s in range(6)]
    for s in range(6):
        near[s:s + 1, :] = met[pl.ds(block_of[s], 1), :]

    def factor(s, t, start, size):
        at = pl.ds(pl.multiple_of(start, 128), size)
        a = near[s:s + 1, at]
        b = near[t:t + 1, at]
        row = core * ROWS + start + lax.broadcasted_iota(jnp.int32, (1, size), 1)
        live = row < jnp.minimum(count_of[s], count_of[t])
        return live, a * b * NG ** (-0.5)

    def own_part(k, _):
        start = pl.multiple_of(k * OWN_PART, 128)
        at = pl.ds(start, OWN_PART)
        for index, (i, j) in enumerate(((0, 0), (0, 1), (1, 1))):
            left = jnp.dot(mix_own[index], own[j, :, at], preferred_element_type=F32)
            density = jnp.sum(left * own[i, :, at].astype(F32), axis=0, keepdims=True)
            live, scale = factor(2 + i, 2 + j, start, OWN_PART)
            weight_own[pl.ds(index, 1), at] = jnp.where(live, scale * density, 0.0)
        return 0

    lax.fori_loop(0, ROWS // OWN_PART, own_part, 0)

    for e in range(2):
        @for_side(e)
        def _():
            k_copy(1 - e).wait_recv()
            k_forward(e).start()

    for e in range(2):
        @for_side(e)
        def _():
            pltpu.make_async_remote_copy(
                src_ref=got_k.at[e, core],
                dst_ref=got_k.at[e, 1 - core],
                send_sem=kf_send.at[e],
                recv_sem=kf_recv.at[e],
                device_id=twin,
                device_id_type=MESH,
            ).wait_recv()

        for j in range(2):
            turned = across(wide_eye, got_k[e, j])
            for i in range(2):
                at = pl.ds(i * NG, NG)
                mix[e, j, at, :] = (sums[6 * i + 4 * e + j] + turned[i * NG:(i + 1) * NG]).astype(BF16)

    acc[...] = jnp.zeros_like(acc)

    def put(e, slot, size, value):
        high = value.astype(BF16)
        zs[e, slot, 0, :, 0:size] = high
        zs[e, slot, 1, :, 0:size] = (value - high.astype(F32)).astype(BF16)

    def gram(e, slot, size, rows):
        return across(rows, zs[e, slot, 0, :, 0:size]) + across(rows, zs[e, slot, 1, :, 0:size])

    def weigh(e, start, size):
        mine_at = pl.ds(there(e, start), size)
        at = pl.ds(start, size)
        y = [own[i, :, mine_at].astype(F32) for i in range(2)]
        weights = []
        for j in range(2):
            left = jnp.dot(mix[e, j], got[e, j, :, at], preferred_element_type=F32)
            each = []
            for i in range(2):
                density = jnp.sum(left[i * NG:(i + 1) * NG] * y[i], axis=0, keepdims=True)
                live, scale = factor(2 + i, 4 * e + j, there(e, start), size)
                each.append(jnp.where(live, scale * density, 0.0))
            weights.append(each)
        return weights

    def from_own(start, size):
        at = pl.ds(start, size)
        y = [own[i, :, at].astype(F32) for i in range(2)]
        mine = [weight_own[pl.ds(index, 1), at] for index in range(3)]
        return (2.0 * mine[0] * y[0] + mine[1] * y[1], mine[1] * y[0] + 2.0 * mine[2] * y[1])

    def from_got(e, start, size, weights):
        x = [got[e, j, :, pl.ds(start, size)].astype(F32) for j in range(2)]
        return tuple(weights[0][i] * x[0] + weights[1][i] * x[1] for i in range(2))

    def one_way(e, start, size):
        weights = weigh(e, start, size)
        y = [own[i, :, pl.ds(there(e, start), size)].astype(F32) for i in range(2)]
        for j in range(2):
            put(e, 2 + j, size, weights[j][0] * y[0] + weights[j][1] * y[1])
        a = from_got(e, start, size, weights)
        b = from_own(there(e, start), size)
        for i in range(2):
            put(e, i, size, a[i] + b[i])

    def both_ways(start, size):
        a = from_got(0, start, size, weigh(0, start, size))
        b = from_got(1, start, size, weigh(1, start, size))
        c = from_own(start, size)
        for i in range(2):
            put(0, i, size, a[i] + b[i] + c[i])

    def add_theirs(e, start, size):
        for j in range(2):
            acc[2 + 2 * e + j] += gram(e, 2 + j, size, got[e, j, :, pl.ds(start, size)])

    def add_mine(e, start, size):
        for i in range(2):
            acc[i] += gram(e, i, size, own[i, :, pl.ds(there(e, start), size)])

    keep = pl.ds(pl.multiple_of(core * OUT, 32), OUT)
    give = pl.ds(pl.multiple_of((1 - core) * OUT, 32), OUT)
    swaps = [
        pltpu.make_async_remote_copy(
            src_ref=acc.at[pl.ds(start, 2), give],
            dst_ref=got_pair.at[pl.ds(start, 2)],
            send_sem=pair_send.at[n],
            recv_sem=pair_recv.at[n],
            device_id=twin,
            device_id_type=MESH,
        )
        for n, start in enumerate((2, 4, 0))
    ]

    def step(k, _):
        for e in range(2):
            rows_sent(e, k)

            @pl.when(k + 2 < PARTS)
            def _():
                send_rows(e, k + 2)

            for later in (PARTS, PARTS + 1):
                @pl.when(k + 2 == later)
                def _():
                    send_rows(e, later)

        for e in range(2):
            rows_here(e, k)
            start = pl.multiple_of(k * PART, 128)
            one_way(e, start, PART)
            add_theirs(e, start, PART)
            add_mine(e, start, PART)
        return 0

    lax.fori_loop(0, PARTS, step, 0)

    for k in range(PARTS, COPIES - 1):
        for e in range(2):
            rows_sent(e, k)
            if k + 2 < COPIES:
                send_rows(e, k + 2)
        for e in range(2):
            rows_here(e, k)
            one_way(e, STARTS[k], SIZES[k])
            add_theirs(e, STARTS[k], SIZES[k])
            if k == COPIES - 2:
                swaps[e].start()
            else:
                add_mine(e, STARTS[k], SIZES[k])
    for e in range(2):
        add_mine(e, STARTS[-2], SIZES[-2])

    results = [
        pltpu.make_async_remote_copy(
            src_ref=send_res.at[e],
            dst_ref=got_res.at[1 - e],
            send_sem=res_send.at[e],
            recv_sem=res_recv.at[1 - e],
            device_id=sides[e],
            device_id_type=MESH,
        )
        for e in range(2)
    ]
    norm = AUXB ** (-0.5)
    for e in range(2):
        swaps[e].wait_recv()
        both = [acc[2 + 2 * e + j, keep, :] + got_pair[2 + 2 * e + j] for j in range(2)]
        send_res[e] = jnp.concatenate([(total * norm).astype(BF16) for total in both], axis=1)

        @for_side(e)
        def _():
            results[e].start()

    for e in range(2):
        rows_sent(e, COPIES - 1)
        rows_here(e, COPIES - 1)
    both_ways(STARTS[-1], BOTH)
    add_mine(0, STARTS[-1], BOTH)
    swaps[2].start()
    swaps[2].wait_recv()
    for i in range(2):
        out[i] = (acc[i, keep, :] + got_pair[i]) * norm
    for e in range(2):
        @for_side(e)
        def _():
            results[1 - e].wait_recv()

        for i in range(2):
            out[i] += got_res[e, :, i * NG:(i + 1) * NG].astype(F32)
    for e in range(2):
        @for_side(e)
        def _():
            k_copy(e).wait_send()
            k_forward(e).wait_send()
            results[e].wait_send()

    for swap in swaps:
        swap.wait_send()


def shards(coeffs, kernel, metric, counts, pairs):
    anywhere = pl.BlockSpec(memory_space=pl.ANY)
    scalars = pl.BlockSpec(memory_space=pltpu.SMEM)
    dma = pltpu.SemaphoreType.DMA
    return pl.pallas_call(
        body,
        out_shape=jax.ShapeDtypeStruct((2, OUT, NG), F32),
        in_specs=[anywhere, anywhere, anywhere, scalars, scalars],
        out_specs=pl.BlockSpec(memory_space=pltpu.VMEM),
        scratch_shapes=[
            pltpu.VMEM((2, NG, ROWS), BF16),
            pltpu.VMEM((2, 2, NG, ONE + BOTH), BF16),
            pltpu.VMEM((PAIRS, NG, NG), BF16),
            pltpu.VMEM((NBLK, ROWS), F32),
            pltpu.VMEM((8, ROWS), F32),
            pltpu.VMEM((12, NG, NG), F32),
            pltpu.VMEM((2, NG, 2 * NG), BF16),
            pltpu.VMEM((2, 2, NG, 2 * NG), BF16),
            pltpu.VMEM((2, 2, 2 * NG, NG), BF16),
            pltpu.VMEM((3, NG, NG), BF16),
            pltpu.VMEM((8, ROWS), F32),
            pltpu.VMEM((2, 4, 2, NG, PART), BF16),
            pltpu.VMEM((6, NG, NG), F32),
            pltpu.VMEM((6, OUT, NG), F32),
            pltpu.VMEM((2, OUT, 2 * NG), BF16),
            pltpu.VMEM((2, OUT, 2 * NG), BF16),
            dma((3,)),
            dma((2, COPIES)),
            dma((2, COPIES)),
            dma((2,)),
            dma((2,)),
            dma((2,)),
            dma((2,)),
            dma((3,)),
            dma((3,)),
            dma((2,)),
            dma((2,)),
        ],
        compiler_params=pltpu.CompilerParams(
            collective_id=0, has_side_effects=True, vmem_limit_bytes=58 * 2 ** 20
        ),
        cost_estimate=pl.CostEstimate(
            flops=30 * 10 ** 9, bytes_accessed=14 * 10 ** 6, transcendentals=0
        ),
    )(jnp.transpose(coeffs, (0, 2, 1)), kernel, metric, counts, jnp.transpose(pairs))


def solution(mesh):
    in_specs = (
        P("curve", "aux", None),
        P("curve", None, None),
        P(None, "aux"),
        P(),
        P("curve", None),
    )
    out_specs = P("curve", "aux", None)
    return jax.shard_map(shards, mesh=mesh, in_specs=in_specs, out_specs=out_specs, check_vma=False)
```

```python
import functools

import jax
import jax.numpy as jnp
from jax import lax
from jax.experimental import pallas as pl
from jax.experimental.pallas import tpu as pltpu
from jax.sharding import PartitionSpec as P

MESH = pl.DeviceIdType.MESH
NG = 320
AUXB = 12800
ROWS = 6400
BOTH = 256
ONE = (ROWS - BOTH) // 2
PART = 512
PARTS = 5
OWN_PART = 640
LAST = (384, 128)
SIZES = (PART,) * PARTS + LAST + (BOTH,)
STARTS = tuple(sum(SIZES[:k]) for k in range(len(SIZES)))
COPIES = len(SIZES)
PAIRS = 8
RING = 64
NBLK = 128
OUT = NG // 2
F32 = jnp.float32
BF16 = jnp.bfloat16


def across(a, b):
    return lax.dot_general(a, b, (((1,), (1,)), ((), ())), preferred_element_type=F32)


def body(
    coeffs, kernel, metric, counts, pairs, out,
    own, got, blocks, met, near, sums, sent_k, got_k, mix, mix_own, weight_own, zs, acc,
    got_pair, send_res, got_res,
    load_sem, row_send, row_recv, k_send, k_recv, kf_send, kf_recv,
    pair_send, pair_recv, res_send, res_recv,
):
    here = lax.axis_index("curve")
    core = lax.axis_index("aux")
    after = lax.rem(here + 1, RING)
    before = lax.rem(here + RING - 1, RING)
    sides = ((before, core), (after, core))
    twin = (here, 1 - core)
    there_is = (here > 0, here < RING - 1)

    def for_side(e):
        return pl.when(there_is[e])


    barrier = pltpu.get_barrier_semaphore()
    pl.semaphore_signal(barrier, inc=1, device_id=twin, device_id_type=MESH)
    for e in range(2):
        @for_side(e)
        def _():
            pl.semaphore_signal(barrier, inc=1, device_id=sides[e], device_id_type=MESH)

    loads = [
        pltpu.make_async_copy(kernel, blocks, load_sem.at[0]),
        pltpu.make_async_copy(metric, met, load_sem.at[1]),
        pltpu.make_async_copy(coeffs, own, load_sem.at[2]),
    ]
    for load in loads:
        load.start()

    for e in range(2):
        @pl.when(jnp.logical_not(there_is[e]))
        def _():
            got[e] = jnp.zeros_like(got[e])
            got_k[e] = jnp.zeros_like(got_k[e])
            got_res[e] = jnp.zeros_like(got_res[e])

    pl.semaphore_wait(barrier, 1 + there_is[0].astype(jnp.int32) + there_is[1].astype(jnp.int32))

    def k_copy(e):
        return pltpu.make_async_remote_copy(
            src_ref=sent_k.at[e],
            dst_ref=got_k.at[1 - e, core],
            send_sem=k_send.at[e],
            recv_sem=k_recv.at[1 - e],
            device_id=sides[e],
            device_id_type=MESH,
        )

    def k_forward(e):
        return pltpu.make_async_remote_copy(
            src_ref=got_k.at[e, core],
            dst_ref=got_k.at[e, core],
            send_sem=kf_send.at[e],
            recv_sem=kf_recv.at[e],
            device_id=twin,
            device_id_type=MESH,
        )

    def there(e, start):
        if isinstance(start, int):
            return start + (ONE + BOTH) * (e == 1 and start < ONE)
        return pl.multiple_of(start + (ONE + BOTH) * e, 128)

    def row_copy(e, k):
        if isinstance(k, int):
            start, size = STARTS[k], SIZES[k]
        else:
            start, size = pl.multiple_of(k * PART, 128), PART
        return pltpu.make_async_remote_copy(
            src_ref=coeffs.at[:, :, pl.ds(there(1 - e, start), size)],
            dst_ref=got.at[1 - e, :, :, pl.ds(start, size)],
            send_sem=row_send.at[e, k],
            recv_sem=row_recv.at[1 - e, k],
            device_id=sides[e],
            device_id_type=MESH,
        )

    def send_rows(e, k):
        @for_side(e)
        def _():
            row_copy(e, k).start()

    def rows_sent(e, k):
        @for_side(e)
        def _():
            row_copy(e, k).wait_send()

    def rows_here(e, k):
        @for_side(e)
        def _():
            row_copy(1 - e, k).wait_recv()

    for e in range(2):
        send_rows(e, 0)
    loads[0].wait()

    first = [pairs[0, p] - 2 * here for p in range(PAIRS)]
    second = [pairs[1, p] - 2 * here + 2 for p in range(PAIRS)]

    def add_kernels(index, _):
        i = index // 6
        s = index % 6
        named = [(first[p] == i) & (second[p] == s) for p in range(PAIRS)]

        def rows(r, _):
            at = pl.ds(pl.multiple_of(r * 64, 64), 64)
            total = jnp.zeros((64, NG), F32)
            for p in range(PAIRS):
                total = total + jnp.where(named[p], blocks[p, at, :].astype(F32), 0.0)
            sums[index, at, :] = total
            return 0

        return lax.fori_loop(0, NG // 64, rows, 0)

    lax.fori_loop(0, 12, add_kernels, 0)


    for e in range(2):
        both = [sums[6 * core + 4 * e + j].astype(BF16) for j in range(2)]
        sent_k[e] = jnp.concatenate(both, axis=1)

        @for_side(e)
        def _():
            k_copy(e).start()

    for e in range(2):
        send_rows(e, 1)

    wide_eye = (
        lax.broadcasted_iota(jnp.int32, (2 * NG, 2 * NG), 0)
        == lax.broadcasted_iota(jnp.int32, (2 * NG, 2 * NG), 1)
    ).astype(BF16)
    eye = wide_eye[:NG, :NG]
    loads[1].wait()
    loads[2].wait()
    mix_own[0] = sums[2].astype(BF16)
    mix_own[2] = sums[9].astype(BF16)
    mix_own[1] = (sums[3] + across(eye, sums[8].astype(BF16))).astype(BF16)

    block_of = [lax.rem(2 * here + NBLK - 2 + s, NBLK) for s in range(6)]
    count_of = [counts[block_of[s]] for s in range(6)]
    for s in range(6):
        near[s:s + 1, :] = met[pl.ds(block_of[s], 1), :]

    def factor(s, t, start, size):
        at = pl.ds(pl.multiple_of(start, 128), size)
        a = near[s:s + 1, at]
        b = near[t:t + 1, at]
        row = core * ROWS + start + lax.broadcasted_iota(jnp.int32, (1, size), 1)
        live = row < jnp.minimum(count_of[s], count_of[t])
        return live, a * b * NG ** (-0.5)

    def own_part(k, _):
        start = pl.multiple_of(k * OWN_PART, 128)
        at = pl.ds(start, OWN_PART)
        for index, (i, j) in enumerate(((0, 0), (0, 1), (1, 1))):
            left = jnp.dot(mix_own[index], own[j, :, at], preferred_element_type=F32)
            density = jnp.sum(left * own[i, :, at].astype(F32), axis=0, keepdims=True)
            live, scale = factor(2 + i, 2 + j, start, OWN_PART)
            weight_own[pl.ds(index, 1), at] = jnp.where(live, scale * density, 0.0)
        return 0

    lax.fori_loop(0, ROWS // OWN_PART, own_part, 0)

    for e in range(2):
        @for_side(e)
        def _():
            k_copy(1 - e).wait_recv()
            k_forward(e).start()

    for e in range(2):
        @for_side(e)
        def _():
            pltpu.make_async_remote_copy(
                src_ref=got_k.at[e, core],
                dst_ref=got_k.at[e, 1 - core],
                send_sem=kf_send.at[e],
                recv_sem=kf_recv.at[e],
                device_id=twin,
                device_id_type=MESH,
            ).wait_recv()

        for j in range(2):
            turned = across(wide_eye, got_k[e, j])
            for i in range(2):
                at = pl.ds(i * NG, NG)
                mix[e, j, at, :] = (sums[6 * i + 4 * e + j] + turned[i * NG:(i + 1) * NG]).astype(BF16)

    acc[...] = jnp.zeros_like(acc)

    def put(e, slot, size, value):
        high = value.astype(BF16)
        zs[e, slot, 0, :, 0:size] = high
        zs[e, slot, 1, :, 0:size] = (value - high.astype(F32)).astype(BF16)

    def gram(e, slot, size, rows):
        return across(rows, zs[e, slot, 0, :, 0:size]) + across(rows, zs[e, slot, 1, :, 0:size])

    def weigh(e, start, size):
        mine_at = pl.ds(there(e, start), size)
        at = pl.ds(start, size)
        y = [own[i, :, mine_at].astype(F32) for i in range(2)]
        weights = []
        for j in range(2):
            left = jnp.dot(mix[e, j], got[e, j, :, at], preferred_element_type=F32)
            each = []
            for i in range(2):
                density = jnp.sum(left[i * NG:(i + 1) * NG] * y[i], axis=0, keepdims=True)
                live, scale = factor(2 + i, 4 * e + j, there(e, start), size)
                each.append(jnp.where(live, scale * density, 0.0))
            weights.append(each)
        return weights

    def from_own(start, size):
        at = pl.ds(start, size)
        y = [own[i, :, at].astype(F32) for i in range(2)]
        mine = [weight_own[pl.ds(index, 1), at] for index in range(3)]
        return (2.0 * mine[0] * y[0] + mine[1] * y[1], mine[1] * y[0] + 2.0 * mine[2] * y[1])

    def from_got(e, start, size, weights):
        x = [got[e, j, :, pl.ds(start, size)].astype(F32) for j in range(2)]
        return tuple(weights[0][i] * x[0] + weights[1][i] * x[1] for i in range(2))

    def one_way(e, start, size):
        weights = weigh(e, start, size)
        y = [own[i, :, pl.ds(there(e, start), size)].astype(F32) for i in range(2)]
        for j in range(2):
            put(e, 2 + j, size, weights[j][0] * y[0] + weights[j][1] * y[1])
        a = from_got(e, start, size, weights)
        b = from_own(there(e, start), size)
        for i in range(2):
            put(e, i, size, a[i] + b[i])

    def both_ways(start, size):
        a = from_got(0, start, size, weigh(0, start, size))
        b = from_got(1, start, size, weigh(1, start, size))
        c = from_own(start, size)
        for i in range(2):
            put(0, i, size, a[i] + b[i] + c[i])

    def add_theirs(e, start, size):
        for j in range(2):
            acc[2 + 2 * e + j] += gram(e, 2 + j, size, got[e, j, :, pl.ds(start, size)])

    def add_mine(e, start, size):
        for i in range(2):
            acc[i] += gram(e, i, size, own[i, :, pl.ds(there(e, start), size)])

    keep = pl.ds(pl.multiple_of(core * OUT, 32), OUT)
    give = pl.ds(pl.multiple_of((1 - core) * OUT, 32), OUT)
    swaps = [
        pltpu.make_async_remote_copy(
            src_ref=acc.at[pl.ds(start, 2), give],
            dst_ref=got_pair.at[pl.ds(start, 2)],
            send_sem=pair_send.at[n],
            recv_sem=pair_recv.at[n],
            device_id=twin,
            device_id_type=MESH,
        )
        for n, start in enumerate((2, 4, 0))
    ]

    def step(k, _):
        for e in range(2):
            rows_sent(e, k)

            @pl.when(k + 2 < PARTS)
            def _():
                send_rows(e, k + 2)

            for later in (PARTS, PARTS + 1):
                @pl.when(k + 2 == later)
                def _():
                    send_rows(e, later)

        for e in range(2):
            rows_here(e, k)
            start = pl.multiple_of(k * PART, 128)
            one_way(e, start, PART)
            add_theirs(e, start, PART)
            add_mine(e, start, PART)
        return 0

    lax.fori_loop(0, PARTS, step, 0)

    for k in range(PARTS, COPIES - 1):
        for e in range(2):
            rows_sent(e, k)
            if k + 2 < COPIES:
                send_rows(e, k + 2)
        for e in range(2):
            rows_here(e, k)
            one_way(e, STARTS[k], SIZES[k])
            add_theirs(e, STARTS[k], SIZES[k])
            if k == COPIES - 2:
                swaps[e].start()
            else:
                add_mine(e, STARTS[k], SIZES[k])

    results = [
        pltpu.make_async_remote_copy(
            src_ref=send_res.at[e],
            dst_ref=got_res.at[1 - e],
            send_sem=res_send.at[e],
            recv_sem=res_recv.at[1 - e],
            device_id=sides[e],
            device_id_type=MESH,
        )
        for e in range(2)
    ]
    norm = AUXB ** (-0.5)
    for e in range(2):
        swaps[e].wait_recv()
        both = [acc[2 + 2 * e + j, keep, :] + got_pair[2 + 2 * e + j] for j in range(2)]
        send_res[e] = jnp.concatenate([(total * norm).astype(BF16) for total in both], axis=1)

        @for_side(e)
        def _():
            results[e].start()

    for e in range(2):
        add_mine(e, STARTS[-2], SIZES[-2])
    for e in range(2):
        rows_sent(e, COPIES - 1)
        rows_here(e, COPIES - 1)
    both_ways(STARTS[-1], BOTH)
    add_mine(0, STARTS[-1], BOTH)
    swaps[2].start()
    swaps[2].wait_recv()
    for i in range(2):
        out[i] = (acc[i, keep, :] + got_pair[i]) * norm
    for e in range(2):
        @for_side(e)
        def _():
            results[1 - e].wait_recv()

        for i in range(2):
            out[i] += got_res[e, :, i * NG:(i + 1) * NG].astype(F32)
    for e in range(2):
        @for_side(e)
        def _():
            k_copy(e).wait_send()
            k_forward(e).wait_send()
            results[e].wait_send()

    for swap in swaps:
        swap.wait_send()


def shards(coeffs, kernel, metric, counts, pairs):
    anywhere = pl.BlockSpec(memory_space=pl.ANY)
    scalars = pl.BlockSpec(memory_space=pltpu.SMEM)
    dma = pltpu.SemaphoreType.DMA
    return pl.pallas_call(
        body,
        out_shape=pltpu.VMEM((2, OUT, NG), F32),
        in_specs=[anywhere, anywhere, anywhere, scalars, scalars],
        out_specs=pl.BlockSpec(memory_space=pltpu.VMEM),
        scratch_shapes=[
            pltpu.VMEM((2, NG, ROWS), BF16),
            pltpu.VMEM((2, 2, NG, ONE + BOTH), BF16),
            pltpu.VMEM((PAIRS, NG, NG), BF16),
            pltpu.VMEM((NBLK, ROWS), F32),
            pltpu.VMEM((8, ROWS), F32),
            pltpu.VMEM((12, NG, NG), F32),
            pltpu.VMEM((2, NG, 2 * NG), BF16),
            pltpu.VMEM((2, 2, NG, 2 * NG), BF16),
            pltpu.VMEM((2, 2, 2 * NG, NG), BF16),
            pltpu.VMEM((3, NG, NG), BF16),
            pltpu.VMEM((8, ROWS), F32),
            pltpu.VMEM((2, 4, 2, NG, PART), BF16),
            pltpu.VMEM((6, NG, NG), F32),
            pltpu.VMEM((6, OUT, NG), F32),
            pltpu.VMEM((2, OUT, 2 * NG), BF16),
            pltpu.VMEM((2, OUT, 2 * NG), BF16),
            dma((3,)),
            dma((2, COPIES)),
            dma((2, COPIES)),
            dma((2,)),
            dma((2,)),
            dma((2,)),
            dma((2,)),
            dma((3,)),
            dma((3,)),
            dma((2,)),
            dma((2,)),
        ],
        compiler_params=pltpu.CompilerParams(
            collective_id=0, has_side_effects=True, vmem_limit_bytes=58 * 2 ** 20
        ),
        cost_estimate=pl.CostEstimate(
            flops=30 * 10 ** 9, bytes_accessed=14 * 10 ** 6, transcendentals=0
        ),
    )(jnp.transpose(coeffs, (0, 2, 1)), kernel, metric, counts, jnp.transpose(pairs))


def solution(mesh):
    in_specs = (
        P("curve", "aux", None),
        P("curve", None, None),
        P(None, "aux"),
        P(),
        P("curve", None),
    )
    out_specs = P("curve", "aux", None)
    return jax.shard_map(shards, mesh=mesh, in_specs=in_specs, out_specs=out_specs, check_vma=False)
```

```python
import functools

import jax
import jax.numpy as jnp
from jax import lax
from jax.experimental import pallas as pl
from jax.experimental.pallas import tpu as pltpu
from jax.sharding import PartitionSpec as P

MESH = pl.DeviceIdType.MESH
NG = 320
AUXB = 12800
ROWS = 6400
BOTH = 256
ONE = (ROWS - BOTH) // 2
PART = 512
PARTS = 5
OWN_PART = 640
LAST = (384, 128)
SIZES = (PART,) * PARTS + LAST + (BOTH,)
STARTS = tuple(sum(SIZES[:k]) for k in range(len(SIZES)))
COPIES = len(SIZES)
PAIRS = 8
RING = 64
NBLK = 128
OUT = NG // 2
F32 = jnp.float32
BF16 = jnp.bfloat16


def across(a, b):
    return lax.dot_general(a, b, (((1,), (1,)), ((), ())), preferred_element_type=F32)


def body(
    coeffs, kernel, metric, counts_in, pairs_in, out,
    counts, pairs,
    own, got, blocks, met, near, sums, sent_k, got_k, mix, mix_own, weight_own, zs, acc,
    got_pair, send_res, got_res,
    load_sem, row_send, row_recv, k_send, k_recv, kf_send, kf_recv,
    pair_send, pair_recv, res_send, res_recv,
):
    here = lax.axis_index("curve")
    core = lax.axis_index("aux")
    after = lax.rem(here + 1, RING)
    before = lax.rem(here + RING - 1, RING)
    sides = ((before, core), (after, core))
    twin = (here, 1 - core)
    there_is = (here > 0, here < RING - 1)

    def for_side(e):
        return pl.when(there_is[e])


    barrier = pltpu.get_barrier_semaphore()
    pl.semaphore_signal(barrier, inc=1, device_id=twin, device_id_type=MESH)
    for e in range(2):
        @for_side(e)
        def _():
            pl.semaphore_signal(barrier, inc=1, device_id=sides[e], device_id_type=MESH)

    for e in range(2):
        @pl.when(jnp.logical_not(there_is[e]))
        def _():
            got[e] = jnp.zeros_like(got[e])
            got_k[e] = jnp.zeros_like(got_k[e])
            got_res[e] = jnp.zeros_like(got_res[e])

    pl.semaphore_wait(barrier, 1 + there_is[0].astype(jnp.int32) + there_is[1].astype(jnp.int32))

    def k_copy(e):
        return pltpu.make_async_remote_copy(
            src_ref=sent_k.at[e],
            dst_ref=got_k.at[1 - e, core],
            send_sem=k_send.at[e],
            recv_sem=k_recv.at[1 - e],
            device_id=sides[e],
            device_id_type=MESH,
        )

    def k_forward(e):
        return pltpu.make_async_remote_copy(
            src_ref=got_k.at[e, core],
            dst_ref=got_k.at[e, core],
            send_sem=kf_send.at[e],
            recv_sem=kf_recv.at[e],
            device_id=twin,
            device_id_type=MESH,
        )

    def there(e, start):
        if isinstance(start, int):
            return start + (ONE + BOTH) * (e == 1 and start < ONE)
        return pl.multiple_of(start + (ONE + BOTH) * e, 128)

    def row_copy(e, k):
        if isinstance(k, int):
            start, size = STARTS[k], SIZES[k]
        else:
            start, size = pl.multiple_of(k * PART, 128), PART
        return pltpu.make_async_remote_copy(
            src_ref=coeffs.at[:, :, pl.ds(there(1 - e, start), size)],
            dst_ref=got.at[1 - e, :, :, pl.ds(start, size)],
            send_sem=row_send.at[e, k],
            recv_sem=row_recv.at[1 - e, k],
            device_id=sides[e],
            device_id_type=MESH,
        )

    def send_rows(e, k):
        @for_side(e)
        def _():
            row_copy(e, k).start()

    def rows_sent(e, k):
        @for_side(e)
        def _():
            row_copy(e, k).wait_send()

    def rows_here(e, k):
        @for_side(e)
        def _():
            row_copy(1 - e, k).wait_recv()

    for e in range(2):
        send_rows(e, 0)
    loads = [
        pltpu.make_async_copy(kernel, blocks, load_sem.at[0]),
        pltpu.make_async_copy(metric, met, load_sem.at[1]),
        pltpu.make_async_copy(coeffs, own, load_sem.at[2]),
        pltpu.make_async_copy(pairs_in, pairs, load_sem.at[3]),
        pltpu.make_async_copy(counts_in, counts, load_sem.at[4]),
    ]
    for load in loads:
        load.start()
    loads[0].wait()
    loads[3].wait()

    first = [pairs[0, p] - 2 * here for p in range(PAIRS)]
    second = [pairs[1, p] - 2 * here + 2 for p in range(PAIRS)]

    def add_kernels(index, _):
        i = index // 6
        s = index % 6
        named = [(first[p] == i) & (second[p] == s) for p in range(PAIRS)]

        def rows(r, _):
            at = pl.ds(pl.multiple_of(r * 64, 64), 64)
            total = jnp.zeros((64, NG), F32)
            for p in range(PAIRS):
                total = total + jnp.where(named[p], blocks[p, at, :].astype(F32), 0.0)
            sums[index, at, :] = total
            return 0

        return lax.fori_loop(0, NG // 64, rows, 0)

    lax.fori_loop(0, 12, add_kernels, 0)


    for e in range(2):
        both = [sums[6 * core + 4 * e + j].astype(BF16) for j in range(2)]
        sent_k[e] = jnp.concatenate(both, axis=1)

        @for_side(e)
        def _():
            k_copy(e).start()

    for e in range(2):
        send_rows(e, 1)

    wide_eye = (
        lax.broadcasted_iota(jnp.int32, (2 * NG, 2 * NG), 0)
        == lax.broadcasted_iota(jnp.int32, (2 * NG, 2 * NG), 1)
    ).astype(BF16)
    eye = wide_eye[:NG, :NG]
    loads[1].wait()
    loads[4].wait()
    loads[2].wait()
    mix_own[0] = sums[2].astype(BF16)
    mix_own[2] = sums[9].astype(BF16)
    mix_own[1] = (sums[3] + across(eye, sums[8].astype(BF16))).astype(BF16)

    block_of = [lax.rem(2 * here + NBLK - 2 + s, NBLK) for s in range(6)]
    count_of = [counts[block_of[s]] for s in range(6)]
    for s in range(6):
        near[s:s + 1, :] = met[pl.ds(block_of[s], 1), :]

    def factor(s, t, start, size):
        at = pl.ds(pl.multiple_of(start, 128), size)
        a = near[s:s + 1, at]
        b = near[t:t + 1, at]
        row = core * ROWS + start + lax.broadcasted_iota(jnp.int32, (1, size), 1)
        live = row < jnp.minimum(count_of[s], count_of[t])
        return live, a * b * NG ** (-0.5)

    def own_part(k, _):
        start = pl.multiple_of(k * OWN_PART, 128)
        at = pl.ds(start, OWN_PART)
        for index, (i, j) in enumerate(((0, 0), (0, 1), (1, 1))):
            left = jnp.dot(mix_own[index], own[j, :, at], preferred_element_type=F32)
            density = jnp.sum(left * own[i, :, at].astype(F32), axis=0, keepdims=True)
            live, scale = factor(2 + i, 2 + j, start, OWN_PART)
            weight_own[pl.ds(index, 1), at] = jnp.where(live, scale * density, 0.0)
        return 0

    lax.fori_loop(0, ROWS // OWN_PART, own_part, 0)

    for e in range(2):
        @for_side(e)
        def _():
            k_copy(1 - e).wait_recv()
            k_forward(e).start()

    for e in range(2):
        @for_side(e)
        def _():
            pltpu.make_async_remote_copy(
                src_ref=got_k.at[e, core],
                dst_ref=got_k.at[e, 1 - core],
                send_sem=kf_send.at[e],
                recv_sem=kf_recv.at[e],
                device_id=twin,
                device_id_type=MESH,
            ).wait_recv()

        for j in range(2):
            turned = across(wide_eye, got_k[e, j])
            for i in range(2):
                at = pl.ds(i * NG, NG)
                mix[e, j, at, :] = (sums[6 * i + 4 * e + j] + turned[i * NG:(i + 1) * NG]).astype(BF16)

    acc[...] = jnp.zeros_like(acc)

    def put(e, slot, size, value):
        high = value.astype(BF16)
        zs[e, slot, 0, :, 0:size] = high
        zs[e, slot, 1, :, 0:size] = (value - high.astype(F32)).astype(BF16)

    def gram(e, slot, size, rows):
        return across(rows, zs[e, slot, 0, :, 0:size]) + across(rows, zs[e, slot, 1, :, 0:size])

    def weigh(e, start, size):
        mine_at = pl.ds(there(e, start), size)
        at = pl.ds(start, size)
        y = [own[i, :, mine_at].astype(F32) for i in range(2)]
        weights = []
        for j in range(2):
            left = jnp.dot(mix[e, j], got[e, j, :, at], preferred_element_type=F32)
            each = []
            for i in range(2):
                density = jnp.sum(left[i * NG:(i + 1) * NG] * y[i], axis=0, keepdims=True)
                live, scale = factor(2 + i, 4 * e + j, there(e, start), size)
                each.append(jnp.where(live, scale * density, 0.0))
            weights.append(each)
        return weights

    def from_own(start, size):
        at = pl.ds(start, size)
        y = [own[i, :, at].astype(F32) for i in range(2)]
        mine = [weight_own[pl.ds(index, 1), at] for index in range(3)]
        return (2.0 * mine[0] * y[0] + mine[1] * y[1], mine[1] * y[0] + 2.0 * mine[2] * y[1])

    def from_got(e, start, size, weights):
        x = [got[e, j, :, pl.ds(start, size)].astype(F32) for j in range(2)]
        return tuple(weights[0][i] * x[0] + weights[1][i] * x[1] for i in range(2))

    def one_way(e, start, size):
        weights = weigh(e, start, size)
        y = [own[i, :, pl.ds(there(e, start), size)].astype(F32) for i in range(2)]
        for j in range(2):
            put(e, 2 + j, size, weights[j][0] * y[0] + weights[j][1] * y[1])
        a = from_got(e, start, size, weights)
        b = from_own(there(e, start), size)
        for i in range(2):
            put(e, i, size, a[i] + b[i])

    def both_ways(start, size):
        a = from_got(0, start, size, weigh(0, start, size))
        b = from_got(1, start, size, weigh(1, start, size))
        c = from_own(start, size)
        for i in range(2):
            put(0, i, size, a[i] + b[i] + c[i])

    def add_theirs(e, start, size):
        for j in range(2):
            acc[2 + 2 * e + j] += gram(e, 2 + j, size, got[e, j, :, pl.ds(start, size)])

    def add_mine(e, start, size):
        for i in range(2):
            acc[i] += gram(e, i, size, own[i, :, pl.ds(there(e, start), size)])

    keep = pl.ds(pl.multiple_of(core * OUT, 32), OUT)
    give = pl.ds(pl.multiple_of((1 - core) * OUT, 32), OUT)
    swaps = [
        pltpu.make_async_remote_copy(
            src_ref=acc.at[pl.ds(start, 2), give],
            dst_ref=got_pair.at[pl.ds(start, 2)],
            send_sem=pair_send.at[n],
            recv_sem=pair_recv.at[n],
            device_id=twin,
            device_id_type=MESH,
        )
        for n, start in enumerate((2, 4, 0))
    ]

    def step(k, _):
        for e in range(2):
            rows_sent(e, k)

            @pl.when(k + 2 < PARTS)
            def _():
                send_rows(e, k + 2)

            for later in (PARTS, PARTS + 1):
                @pl.when(k + 2 == later)
                def _():
                    send_rows(e, later)

        for e in range(2):
            rows_here(e, k)
            start = pl.multiple_of(k * PART, 128)
            one_way(e, start, PART)
            add_theirs(e, start, PART)
            add_mine(e, start, PART)
        return 0

    lax.fori_loop(0, PARTS, step, 0)

    for k in range(PARTS, COPIES - 1):
        for e in range(2):
            rows_sent(e, k)
            if k + 2 < COPIES:
                send_rows(e, k + 2)
        for e in range(2):
            rows_here(e, k)
            one_way(e, STARTS[k], SIZES[k])
            add_theirs(e, STARTS[k], SIZES[k])
            if k == COPIES - 2:
                swaps[e].start()
            else:
                add_mine(e, STARTS[k], SIZES[k])

    results = [
        pltpu.make_async_remote_copy(
            src_ref=send_res.at[e],
            dst_ref=got_res.at[1 - e],
            send_sem=res_send.at[e],
            recv_sem=res_recv.at[1 - e],
            device_id=sides[e],
            device_id_type=MESH,
        )
        for e in range(2)
    ]
    norm = AUXB ** (-0.5)
    for e in range(2):
        swaps[e].wait_recv()
        both = [acc[2 + 2 * e + j, keep, :] + got_pair[2 + 2 * e + j] for j in range(2)]
        send_res[e] = jnp.concatenate([(total * norm).astype(BF16) for total in both], axis=1)

        @for_side(e)
        def _():
            results[e].start()

    for e in range(2):
        add_mine(e, STARTS[-2], SIZES[-2])
    for e in range(2):
        rows_sent(e, COPIES - 1)
        rows_here(e, COPIES - 1)
    both_ways(STARTS[-1], BOTH)
    add_mine(0, STARTS[-1], BOTH)
    swaps[2].start()
    swaps[2].wait_recv()
    for i in range(2):
        out[i] = (acc[i, keep, :] + got_pair[i]) * norm
    for e in range(2):
        @for_side(e)
        def _():
            results[1 - e].wait_recv()

        for i in range(2):
            out[i] += got_res[e, :, i * NG:(i + 1) * NG].astype(F32)
    for e in range(2):
        @for_side(e)
        def _():
            k_copy(e).wait_send()
            k_forward(e).wait_send()
            results[e].wait_send()

    for swap in swaps:
        swap.wait_send()


def shards(coeffs, kernel, metric, counts, pairs):
    anywhere = pl.BlockSpec(memory_space=pl.ANY)
    dma = pltpu.SemaphoreType.DMA
    return pl.pallas_call(
        body,
        out_shape=pltpu.VMEM((2, OUT, NG), F32),
        in_specs=[anywhere] * 5,
        out_specs=pl.BlockSpec(memory_space=pltpu.VMEM),
        scratch_shapes=[
            pltpu.SMEM((NBLK,), jnp.int32),
            pltpu.SMEM((2, PAIRS), jnp.int32),
            pltpu.VMEM((2, NG, ROWS), BF16),
            pltpu.VMEM((2, 2, NG, ONE + BOTH), BF16),
            pltpu.VMEM((PAIRS, NG, NG), BF16),
            pltpu.VMEM((NBLK, ROWS), F32),
            pltpu.VMEM((8, ROWS), F32),
            pltpu.VMEM((12, NG, NG), F32),
            pltpu.VMEM((2, NG, 2 * NG), BF16),
            pltpu.VMEM((2, 2, NG, 2 * NG), BF16),
            pltpu.VMEM((2, 2, 2 * NG, NG), BF16),
            pltpu.VMEM((3, NG, NG), BF16),
            pltpu.VMEM((8, ROWS), F32),
            pltpu.VMEM((2, 4, 2, NG, PART), BF16),
            pltpu.VMEM((6, NG, NG), F32),
            pltpu.VMEM((6, OUT, NG), F32),
            pltpu.VMEM((2, OUT, 2 * NG), BF16),
            pltpu.VMEM((2, OUT, 2 * NG), BF16),
            dma((5,)),
            dma((2, COPIES)),
            dma((2, COPIES)),
            dma((2,)),
            dma((2,)),
            dma((2,)),
            dma((2,)),
            dma((3,)),
            dma((3,)),
            dma((2,)),
            dma((2,)),
        ],
        compiler_params=pltpu.CompilerParams(
            collective_id=0, has_side_effects=True, vmem_limit_bytes=58 * 2 ** 20
        ),
        cost_estimate=pl.CostEstimate(
            flops=30 * 10 ** 9, bytes_accessed=14 * 10 ** 6, transcendentals=0
        ),
    )(jnp.transpose(coeffs, (0, 2, 1)), kernel, metric, counts, jnp.transpose(pairs))


def solution(mesh):
    in_specs = (
        P("curve", "aux", None),
        P("curve", None, None),
        P(None, "aux"),
        P(),
        P("curve", None),
    )
    out_specs = P("curve", "aux", None)
    return jax.shard_map(shards, mesh=mesh, in_specs=in_specs, out_specs=out_specs, check_vma=False)
```
